128 devices in a mesh: partner: 16 (over y, x_lo, core), blk: 8 (over z, x_hi).
Axes of the slice: x: 4 (x_hi: 2, x_lo: 2; x = x_hi * 2 + x_lo), y: 4, z: 4, core: 2. Of those that a mesh axis runs over, the one named last changes fastest.
Arguments:
- tensor_slab: float32 [8, 8192, 4096], P(None, 'partner', 'blk'), may hold values from -6 to 6
- sign_flips: int32 [8192], P('partner'), may hold values from -1 to 1, as said below
- mode2_factor: float32 [4096, 64], P('blk'), may hold values from -6 to 6
- mode3_factor: float32 [8, 64], replicated, may hold values from -6 to 6
- fibre_col: int32 [4096], P('blk'), may hold values from 0 to 511
- fibre_depth: int32 [4096], P('blk'), may hold values from 0 to 7
Outputs:
- mixed_slab: float32 [8, 8192, 4096], P(None, 'partner', 'blk')
- factor_update: float32 [8192, 64], P('partner')
The draws below stay inside these ranges and needn't reach their ends.
Inputs may be any that keep to these rules, and one draw needn't show every extreme that they name: `sign_flips`: every entry is -1 or 1.
All inputs are finite; a program needn't handle non-finite values.
Results may differ from the reference program's by a relative error of at most 0.000098.
Values sent between devices are 32-bit elements; how exact they have to be, the bound alone decides.
No kernel may reach another device: no remote copies, remote signals or barrier semaphores. Data moves between devices by JAX's collectives and lax.ppermute only.
A program may use at most 128 MiB of HBM per device.

```python
import math
import jax
import jax.numpy as jnp
from jax import lax

I = 8192
R = 64
K = 8
JB = 512
S_DEV = 512
J = 4096
TOTAL = 4096


def draw_sign_flips(key, part):
    key = jax.random.fold_in(key, 7)
    return (2 * jax.random.randint(key, (I,), 0, 2) - 1).astype(jnp.int32)


def with_ends(values, own_key, least, top_value):
    place = [jax.random.randint(jax.random.fold_in(own_key, axis), (), 0, length) for axis, length in enumerate(values.shape)]
    widest = values.shape.index(max(values.shape))
    beside = place[:widest] + [(place[widest] + 1) % values.shape[widest]] + place[widest + 1:]
    return values.at[tuple(place)].set(least).at[tuple(beside)].set(top_value)


def block_levels(rng, dims, shards, least, top_value):
    loudness, own = 1.0, jax.random.fold_in(rng, 6)
    for axis_at, parts in shards:
        steps = jnp.exp(jax.random.uniform(jax.random.fold_in(own, axis_at), (parts,), jnp.float32, least / len(shards), top_value / len(shards)))
        loudness = loudness * jnp.repeat(steps, dims[axis_at] // parts).reshape([-1 if axis == axis_at else 1 for axis in range(len(dims))])
    return loudness


def normal_values(own_key, shape, spread, reach, pieces=(), held_as=jnp.bfloat16):
    values = spread * jax.random.normal(own_key, shape, jnp.float32)
    if pieces:
        values = values * block_levels(own_key, shape, pieces, -0.22, 0.18)
    return jnp.clip(values, -reach, reach).astype(held_as)


def setup_inputs(seed: int = 0) -> dict:
    key_list = jax.random.split(jax.random.key(seed), 7)
    tensor_slab = normal_values(key_list[0], (K, I, J), 1.0, 6.0, ((1, 16), (2, 8)), jnp.float32)
    sign_flips = draw_sign_flips(jax.random.fold_in(key_list[6], 71), 0)
    mode2_factor = normal_values(key_list[2], (J, R), 1.0, 6.0, ((0, 8),), jnp.float32)
    mode3_factor = normal_values(key_list[3], (K, R), 1.0, 6.0, (), jnp.float32)
    fibre_col = with_ends(jax.random.randint(key_list[4], (TOTAL,), 0, JB), jax.random.fold_in(key_list[4], 1), 0, JB - 1).astype(jnp.int32)
    fibre_depth = with_ends(jax.random.randint(key_list[5], (TOTAL,), 0, K), jax.random.fold_in(key_list[5], 1), 0, K - 1).astype(jnp.int32)
    return {"tensor_slab": tensor_slab, "sign_flips": sign_flips, "mode2_factor": mode2_factor, "mode3_factor": mode3_factor, "fibre_col": fibre_col, "fibre_depth": fibre_depth}


ridge = 0.1

def walsh_rows(field):
    depth_count, length_all, column_count = field.shape
    stride_len = 1
    while stride_len < length_all:
        shaped = field.reshape(depth_count, length_all // (2 * stride_len), 2, stride_len, column_count)
        upper_part = shaped[:, :, 0]
        lower_part = shaped[:, :, 1]
        field = jnp.stack([upper_part + lower_part, upper_part - lower_part], axis=2).reshape(depth_count, length_all, column_count)
        stride_len = stride_len * 2
    return field

def reference(tensor_slab, sign_flips, mode2_factor, mode3_factor, fibre_col, fibre_depth):
    flipped = tensor_slab * sign_flips.astype(jnp.float32)[None, :, None]
    mixed_slab = walsh_rows(flipped) * (1.0 / math.sqrt(I))
    block_of = (jnp.arange(TOTAL, dtype=jnp.int32) // S_DEV).astype(jnp.int32)
    global_col = (fibre_col + block_of * JB).astype(jnp.int32)
    picked = mixed_slab[fibre_depth, :, global_col]
    khatri = mode2_factor[global_col] * mode3_factor[fibre_depth]
    moment = lax.dot_general(picked, khatri, (((0,), (0,)), ((), ())), precision=lax.Precision.HIGHEST) * (1.0 / math.sqrt(TOTAL))
    gram = lax.dot_general(khatri, khatri, (((0,), (0,)), ((), ())), precision=lax.Precision.HIGHEST) * (1.0 / TOTAL)
    gram = gram + ridge * jnp.eye(R, dtype=jnp.float32)
    factor_update = jnp.linalg.solve(gram, moment.T).T
    return (mixed_slab, factor_update)
```

```python
import functools
import math

import jax
import jax.numpy as jnp
import numpy as np
from jax import lax
from jax.experimental import pallas as pl
from jax.experimental.pallas import tpu as pltpu
from jax.sharding import PartitionSpec as P

ridge = 0.1
HIGH = lax.Precision.HIGHEST


def hadamard(order_len):
    table = np.ones((1, 1), np.float32)
    while table.shape[0] < order_len:
        table = np.block([[table, table], [table, -table]])
    return table


def butterflies(parts):
    stride = 1
    while stride < len(parts):
        parts = [
            parts[i] + parts[i + stride] if not i & stride else parts[i - stride] - parts[i]
            for i in range(len(parts))
        ]
        stride *= 2
    return parts


def middle_kernel(signs_ref, table_ref, x_ref, o_ref):
    table = table_ref[...]
    flipped = [x_ref[p] * signs_ref[p] for p in range(x_ref.shape[0])]
    for p, value in enumerate(butterflies(flipped)):
        high = value.astype(jnp.bfloat16)
        low = (value - high.astype(jnp.float32)).astype(jnp.bfloat16)
        o_ref[p] = jnp.dot(table, high, preferred_element_type=jnp.float32) + jnp.dot(
            table, low, preferred_element_type=jnp.float32
        )


def middle(signs, table, x, tile):
    parties, rows, cols = x.shape
    return pl.pallas_call(
        middle_kernel,
        out_shape=jax.ShapeDtypeStruct(x.shape, jnp.float32),
        grid=(cols // tile,),
        in_specs=[
            pl.BlockSpec((parties, rows, 1), lambda j: (0, 0, 0)),
            pl.BlockSpec((rows, rows), lambda j: (0, 0)),
            pl.BlockSpec((parties, rows, tile), lambda j: (0, 0, j)),
        ],
        out_specs=pl.BlockSpec((parties, rows, tile), lambda j: (0, 0, j)),
        compiler_params=pltpu.CompilerParams(vmem_limit_bytes=48 * 2**20),
        cost_estimate=pl.CostEstimate(
            flops=4 * parties * rows * rows * cols, bytes_accessed=8 * x.size, transcendentals=0
        ),
    )(signs, table, x)


def end_kernel(scale, x_ref, o_ref):
    half = x_ref.shape[1] // 2
    upper, lower = x_ref[0, :half] * scale, x_ref[0, half:] * scale
    o_ref[0, :half] = upper + lower
    o_ref[0, half:] = upper - lower


def end(x, scale):
    depth, rows, cols = x.shape
    block = pl.BlockSpec((1, rows, cols), lambda k: (k, 0, 0))
    return pl.pallas_call(
        functools.partial(end_kernel, scale),
        out_shape=jax.ShapeDtypeStruct(x.shape, jnp.float32),
        grid=(depth,),
        in_specs=[block],
        out_specs=block,
        compiler_params=pltpu.CompilerParams(vmem_limit_bytes=32 * 2**20),
        cost_estimate=pl.CostEstimate(flops=3 * x.size, bytes_accessed=8 * x.size, transcendentals=0),
    )(x)


def sample_kernel(col_ref, depth_ref, signs_ref, mode2_ref, mode3_ref, x_ref, o_ref):
    k = pl.program_id(0)
    rows, cols = x_ref.shape[1:]
    chosen = jnp.where(depth_ref[...] == k, col_ref[...], -1)
    hits = lax.broadcasted_iota(jnp.int32, (cols, chosen.shape[1]), 0) == chosen
    count = jnp.sum(hits.astype(jnp.float32), axis=1, keepdims=True)
    khatri = mode2_ref[...] * mode3_ref[0]
    weighted = khatri * count

    @pl.when(k == 0)
    def _():
        o_ref[...] = jnp.zeros_like(o_ref)

    o_ref[:rows] += signs_ref[...] * jnp.dot(
        x_ref[0], weighted, precision=HIGH, preferred_element_type=jnp.float32
    )
    o_ref[rows:] += lax.dot_general(
        khatri, weighted, (((0,), (0,)), ((), ())), precision=HIGH, preferred_element_type=jnp.float32
    )


def sample(col, depth, signs, mode2, mode3, x):
    slices, rows, cols = x.shape
    rank = mode2.shape[1]
    whole = lambda *shape: pl.BlockSpec(shape, lambda k: (0,) * len(shape))
    return pl.pallas_call(
        sample_kernel,
        out_shape=jax.ShapeDtypeStruct((rows + rank, rank), jnp.float32),
        grid=(slices,),
        in_specs=[
            whole(1, col.shape[0]),
            whole(1, col.shape[0]),
            whole(rows, 1),
            whole(cols, rank),
            pl.BlockSpec((1, 1, rank), lambda k: (k, 0, 0)),
            pl.BlockSpec((1, rows, cols), lambda k: (k, 0, 0)),
        ],
        out_specs=whole(rows + rank, rank),
        compiler_params=pltpu.CompilerParams(vmem_limit_bytes=32 * 2**20),
        cost_estimate=pl.CostEstimate(
            flops=12 * x.size * rank, bytes_accessed=4 * x.size, transcendentals=0
        ),
    )(col[None], depth[None], signs[:, None], mode2, mode3[:, None], x)


def solve_normal(gram, moment):
    factor_chol = jnp.linalg.cholesky(gram)
    return jax.scipy.linalg.cho_solve((factor_chol, True), moment.T).T


def shards(tensor_slab, sign_flips, mode2_factor, mode3_factor, fibre_col, fibre_depth):
    slices, rows, cols = tensor_slab.shape
    parties = lax.axis_size("partner")
    me = lax.axis_index("partner")
    rank = mode2_factor.shape[1]
    total = fibre_col.shape[0] * lax.axis_size("blk")
    signs = sign_flips.astype(jnp.float32)
    piece = slices * rows // parties
    halves = rows // piece

    sent = lax.all_to_all(tensor_slab.reshape(parties, piece, cols), "partner", 0, 0)
    all_signs = lax.all_gather(signs, "partner").reshape(parties, halves, piece)
    my_signs = lax.dynamic_index_in_dim(all_signs, me % halves, 1, keepdims=False)
    table = jnp.asarray(hadamard(piece), jnp.bfloat16)
    mixed = middle(my_signs[..., None], table, sent, 128)
    back = lax.all_to_all(mixed, "partner", 0, 0).reshape(slices, rows, cols)
    mixed_slab = end(back, 1.0 / math.sqrt(rows * parties))

    part = sample(fibre_col, fibre_depth, signs, mode2_factor, mode3_factor, tensor_slab)
    summed = lax.psum(part, "blk")
    gram = summed[rows:] * (1.0 / total) + ridge * jnp.eye(rank, dtype=jnp.float32)
    solved = solve_normal(gram, summed[:rows])
    scale = 1.0 / math.sqrt(total) / math.sqrt(rows * parties)
    factor = jnp.dot(jnp.asarray(hadamard(rows)), solved, precision=HIGH) * scale
    for bit in range(parties.bit_length() - 1):
        other = lax.ppermute(factor, "partner", [(s, s ^ (1 << bit)) for s in range(parties)])
        upper = jnp.bitwise_and(jnp.right_shift(me, bit), 1) == 1
        factor = jnp.where(upper, other - factor, factor + other)
    return (mixed_slab, factor)


def solution(mesh):
    return jax.shard_map(
        shards,
        mesh=mesh,
        in_specs=(P(None, "partner", "blk"), P("partner"), P("blk", None), P(), P("blk"), P("blk")),
        out_specs=(P(None, "partner", "blk"), P("partner", None)),
        check_vma=False,
    )
```

```python
import functools
import math

import jax
import jax.numpy as jnp
import numpy as np
from jax import lax
from jax.experimental import pallas as pl
from jax.experimental.pallas import tpu as pltpu
from jax.sharding import PartitionSpec as P

ridge = 0.1
HIGH = lax.Precision.HIGHEST
F32 = jnp.float32
HBM = pl.BlockSpec(memory_space=pltpu.HBM)
COST = 30_000_000
VMEM = pl.BlockSpec(memory_space=pltpu.VMEM)
SMEM = pl.BlockSpec(memory_space=pltpu.SMEM)


def hadamard(order_len):
    table = np.ones((1, 1), np.float32)
    while table.shape[0] < order_len:
        table = np.block([[table, table], [table, -table]])
    return table


def sign_of(bit):
    return (1 - 2 * bit).astype(F32)


def y_signs(place_ref):
    low, high = sign_of(place_ref[0] & 1), sign_of(place_ref[0] >> 1)
    return [jnp.float32(1), low, high, low * high]


def struct(*shape):
    return jax.ShapeDtypeStruct(shape, F32)


class Chain:
    def __init__(self, place):
        self.place, self.mark = place, None

    def __call__(self, body, operands, in_specs, out_shapes, out_specs, aliases=None, scratch=(), grid=(), limit=12, cost=0):
        marks = () if self.mark is None else (self.mark,)
        n_in, n_out = len(operands), len(out_shapes)

        def inner(place_ref, *refs):
            outs = refs[n_in + len(marks):]
            body(place_ref, *refs[:n_in], *outs[:n_out], *outs[n_out + 1:])

        *outs, self.mark = pl.pallas_call(
            inner,
            out_shape=list(out_shapes) + [struct(8, 128)],
            grid=grid,
            in_specs=[SMEM] + list(in_specs) + [HBM] * len(marks),
            out_specs=list(out_specs) + [HBM],
            scratch_shapes=scratch,
            input_output_aliases=aliases or {},
            compiler_params=pltpu.CompilerParams(vmem_limit_bytes=limit * 2**20),
            cost_estimate=pl.CostEstimate(flops=0, bytes_accessed=cost, transcendentals=0),
        )(self.place, *operands, *marks)
        return outs


def by_rows(rows, step, work):
    def one(i, carry):
        work(pl.ds(pl.multiple_of(i * step, step), step))
        return carry

    lax.fori_loop(0, rows // step, one, 0)


def first(chain, slab, signs, table, groups):
    rows, cols = slab.shape[1:]

    def body(place_ref, signs_ref, table_ref, x_ref, *refs):
        o_refs, held, sems = refs[:2], refs[2], refs[3]
        copies = [
            pltpu.make_async_copy(x_ref.at[2 * group + i], held.at[2 * n + i], sems.at[2 * n + i])
            for n, group in enumerate(groups) for i in range(2)
        ]
        for copy in copies:
            copy.start()
        for n, copy in enumerate(copies):
            copy.wait()
            value = held[n] * signs_ref[...]
            high = value.astype(jnp.bfloat16)
            low = (value - high.astype(F32)).astype(jnp.bfloat16)
            o_refs[n // 2][n % 2] = jnp.dot(table_ref[...], high, preferred_element_type=F32) + jnp.dot(
                table_ref[...], low, preferred_element_type=F32
            )

    return chain(
        body, (signs, table, slab), [VMEM, VMEM, HBM], [struct(2, rows, cols)] * 2, [VMEM] * 2,
        scratch=[pltpu.VMEM((4, rows, cols), F32), pltpu.SemaphoreType.DMA((4,))], limit=48,
    )


def combine_split(chain, which, own, other):
    rows, cols = own.shape[1:]
    half = rows // 2

    def body(place_ref, a_ref, b_ref, *o_refs):
        sign = sign_of(place_ref[which])
        for m in range(4):
            piece = place_ref[0] ^ m
            a, b = (ref.at[piece >> 1, pl.ds(pl.multiple_of((piece & 1) * half, half), half)] for ref in (a_ref, b_ref))

            def work(at, a=a, b=b, o=o_refs[m]):
                o[at, :] = b[at, :] + a[at, :] * sign

            by_rows(half, 64, work)

    return chain(body, (own, other), [VMEM] * 2, [struct(half, cols)] * 4, [VMEM] * 4)


def combine_one(chain, which, own, other, k):
    rows, cols = own.shape[1:]

    def body(place_ref, a_ref, b_ref, o_ref):
        sign = sign_of(place_ref[which])

        def work(at):
            o_ref[at, :] = b_ref[k, at, :] + a_ref[k, at, :] * sign

        by_rows(rows, 64, work)

    return chain(body, (own, other), [VMEM] * 2, [struct(rows, cols)], [VMEM])[0]


def combine_split_slices(chain, which, own, other):
    rows, cols = own[0].shape
    half, extra = rows // 2, (own[1].shape[0] - rows) // 4

    def body(place_ref, *refs):
        sign = sign_of(place_ref[which])
        for m in range(4):
            piece = place_ref[0] ^ m
            for k in range(2):
                @pl.when(piece >> 1 == k)
                def _(m=m, k=k, piece=piece):
                    a, b = (ref.at[pl.ds(pl.multiple_of((piece & 1) * half, half), half)] for ref in (refs[k], refs[2 + k]))

                    def work(at):
                        refs[4 + m][at, :] = b[at, :] + a[at, :] * sign

                    by_rows(half, 64, work)

            if extra:
                at = pl.ds(pl.multiple_of(rows + piece * extra, extra), extra)
                refs[4 + m][half:] = refs[3][at, :] + refs[1][at, :] * sign

    return chain(
        body, tuple(own) + tuple(other), [VMEM] * 4, [struct(half + extra, cols)] * 4, [VMEM] * 4
    )


def middle(chain, parts):
    half, cols = parts[0].shape

    def body(place_ref, *refs):
        signs = y_signs(place_ref)

        def work(at):
            a, b, c, d = (refs[m][at, :] * signs[m] for m in range(4))
            s, t, u, v = a + b, a - b, c + d, c - d
            for m, value in enumerate((s + u, t + v, s - u, t - v)):
                refs[4 + m][at, :] = value * (signs[3] * signs[m])

        by_rows(half, 16, work)

    return chain(body, tuple(parts), [VMEM] * 4, [struct(half, cols)] * 4, [VMEM] * 4)


def pack(chain, parts):
    half, cols = parts[0].shape

    def body(place_ref, *refs):
        for m in range(4):
            def work(at, m=m):
                refs[4 + m // 2][m % 2, at, :] = refs[m][at, :]

            by_rows(half, 64, work)

    return chain(body, tuple(parts), [VMEM] * 4, [struct(2, half, cols)] * 2, [VMEM] * 2)


def gate(chain, values, after):
    n = len(values)

    def body(place_ref, *refs):
        for i in range(n):
            flat = refs[i].shape[0] if len(refs[i].shape) == 2 else None

            def work(at, i=i):
                refs[n + len(after) + i][at] = refs[i][at]

            if flat:
                by_rows(flat, 16, work)
            else:
                by_rows(refs[i].shape[0], 1, work)

    return chain(
        body, tuple(values) + tuple(after), [VMEM] * (n + len(after)), [struct(*v.shape) for v in values], [VMEM] * n
    )


def to_place(place_ref, source, out, group, m, half, sem):
    piece = place_ref[0] ^ m
    start = pl.multiple_of((piece & 1) * half, half)
    copy = pltpu.make_async_copy(source, out.at[2 * group + (piece >> 1), pl.ds(start, half), :], sem)
    copy.start()
    return copy


def end_slices(chain, which, own, other, group, shape):
    half, cols = own[0].shape[1:]

    def body(place_ref, *refs):
        out, held, sems = refs[4:]
        sign = sign_of(place_ref[which])
        copies = []
        for m in range(4):
            def work(at, m=m):
                held[m, at, :] = refs[2 + m // 2][m % 2, at, :] + refs[m // 2][m % 2, at, :] * sign

            by_rows(half, 64, work)
            copies.append(to_place(place_ref, held.at[m], out, group, m, half, sems.at[m]))
        for copy in copies:
            copy.wait()

    return chain(
        body, tuple(own) + tuple(other), [VMEM] * 4, [struct(*shape)], [HBM],
        scratch=[pltpu.VMEM((4, half, cols), F32), pltpu.SemaphoreType.DMA((4,))],
    )[0]


def end_mixed(chain, parts, group, which, own, other, other_group, first_piece, buffer, cost):
    half, cols = buffer.shape[1] // 2, buffer.shape[2]
    names = list(parts)
    n, pieces = len(names), 0 if own is None else own.shape[0]
    pair = () if own is None else (own, other)

    def body(place_ref, *refs):
        out, held, sems = refs[n + len(pair) + 1:]
        copies = [to_place(place_ref, refs[i], out, group, m, half, sems.at[i]) for i, m in enumerate(names)]
        for m in range(pieces):
            def work(at, m=m):
                held[m, at, :] = refs[n + 1][m, at, :] + refs[n][m, at, :] * sign_of(place_ref[which])

            by_rows(half, 64, work)
            copies.append(to_place(place_ref, held.at[m], out, other_group, first_piece + m, half, sems.at[n + m]))
        for copy in copies:
            copy.wait()

    return chain(
        body, tuple(parts[m] for m in names) + pair + (buffer,), [VMEM] * (n + len(pair)) + [HBM],
        [struct(*buffer.shape)], [HBM], aliases={n + len(pair) + 1: 0}, cost=cost,
        scratch=[pltpu.VMEM((max(pieces, 1), half, cols), F32), pltpu.SemaphoreType.DMA((n + pieces,))],
    )[0]


def times_inverse(chain, moment, inverse):
    rank, rows = moment.shape

    def body(place_ref, a_ref, inverse_ref, o_ref):
        o_ref[...] = lax.dot_general(
            a_ref[...], inverse_ref[...], (((0,), (0,)), ((), ())), precision=HIGH, preferred_element_type=F32
        )

    return chain(body, (moment, inverse), [VMEM] * 2, [struct(rows, rank)], [VMEM])[0]


def sample(chain, col, depth, signs, mode2, mode3, slab, table, factor):
    slices, rows, cols = slab.shape
    samples, rank = col.shape[1], mode2.shape[1]

    def body(place_ref, col_ref, depth_ref, signs_ref, mode2_ref, mode3_ref, table_ref, x_ref, o_ref, gram_ref, total):
        k = pl.program_id(0)
        khatri = mode2_ref[...] * mode3_ref[0]
        weighted = khatri * counts(col_ref, depth_ref, k, cols)
        part = lax.dot_general(
            weighted, x_ref[0], (((0,), (1,)), ((), ())), precision=HIGH, preferred_element_type=F32
        )

        gram = lax.dot_general(
            khatri, weighted, (((0,), (0,)), ((), ())), precision=HIGH, preferred_element_type=F32
        )

        @pl.when(k == 0)
        def _():
            total[...] = part
            gram_ref[...] = gram

        @pl.when(k > 0)
        def _():
            total[...] += part
            gram_ref[...] += gram

        @pl.when(k == slices - 1)
        def _():
            rest = total[...] * (signs_ref[...] * factor)
            done = jnp.zeros_like(rest)
            for _ in range(3):
                step = rest.astype(jnp.bfloat16)
                rest = rest - step.astype(F32)
                done = done + jnp.dot(step, table_ref[...], preferred_element_type=F32)
            o_ref[...] = done

    whole = lambda *shape: pl.BlockSpec(shape, lambda k: (0,) * len(shape))
    return chain(
        body, (col, depth, signs, mode2, mode3, table, slab),
        [
            whole(1, samples),
            whole(1, samples),
            whole(1, rows),
            whole(cols, rank),
            pl.BlockSpec((1, 1, rank), lambda k: (k, 0, 0)),
            whole(rows, rows),
            pl.BlockSpec((1, rows, cols), lambda k: (k, 0, 0)),
        ],
        [struct(rank, rows), struct(rank, rank)], [whole(rank, rows), whole(rank, rank)],
        scratch=[pltpu.VMEM((rank, rows), F32)], grid=(slices,), limit=16,
    )


def counts(col_ref, depth_ref, k, cols):
    chosen = jnp.where(depth_ref[...] == k, col_ref[...], -1)
    hits = lax.broadcasted_iota(jnp.int32, (cols, chosen.shape[1]), 0) == chosen
    return jnp.sum(hits.astype(F32), axis=1, keepdims=True)


def fold(chain, which, own, other, more=None):
    rows, cols = own.shape
    square = () if more is None else (more,)
    under = 0 if more is None else more.shape[0]

    def body(place_ref, a_ref, b_ref, *refs):
        o_ref = refs[-1]
        o_ref[:rows] = b_ref[...] + a_ref[...] * sign_of(place_ref[which])
        if under:
            o_ref[rows:] = jnp.zeros((under, cols), F32)
            o_ref[rows:, :under] = refs[0][...]

    return chain(body, (own, other) + square, [VMEM] * (2 + len(square)), [struct(rows + under, cols)], [VMEM])[0]


def add(chain, own, other, rows):
    def body(place_ref, a_ref, b_ref, o_ref):
        o_ref[...] = a_ref[:rows] + b_ref[:rows]

    return chain(body, (own, other), [VMEM] * 2, [struct(rows, own.shape[1])], [VMEM])[0]


def inverse_of(chain, summed, rank, total):
    def body(place_ref, x_ref, o_ref, moment_ref, work):
        moment_ref[...] = x_ref[:rank]
        row = lax.broadcasted_iota(jnp.int32, (rank, 2 * rank), 0)
        col = lax.broadcasted_iota(jnp.int32, (rank, 2 * rank), 1)
        square_row, square_col = row[:, :rank], col[:, :rank]
        eye = jnp.where(square_row == square_col, 1.0, 0.0)
        gram = x_ref[rank:, :rank] * (1.0 / total) + ridge * eye
        work[:, :rank] = gram
        work[:, rank:] = eye

        def step(j, carry):
            now = work[...]
            pivot_row = work[pl.ds(j, 1), :]
            pivot = jnp.sum(jnp.where(col[:1] == j, pivot_row, 0.0), axis=1, keepdims=True)
            pivot_row = pivot_row / pivot
            column = jnp.sum(jnp.where(col == j, now, 0.0), axis=1, keepdims=True)
            work[...] = jnp.where(row == j, pivot_row, now - column * pivot_row)
            return carry

        lax.fori_loop(0, rank, step, 0)
        found = work[:, rank:]
        dot = lambda a, b: jnp.dot(a, b, precision=HIGH, preferred_element_type=F32)
        o_ref[...] = found + dot(found, eye - dot(gram, found))

    return chain(
        body, (summed,), [VMEM], [struct(rank, rank), struct(rank, summed.shape[1])], [VMEM] * 2,
        scratch=[pltpu.VMEM((rank, 2 * rank), F32)],
    )


def swap(value, mask, axis="partner"):
    return lax.ppermute(value, axis, [(s, s ^ mask) for s in range(lax.axis_size(axis))])


def shards(tensor_slab, sign_flips, mode2_factor, mode3_factor, fibre_col, fibre_depth):
    slices, rows, cols = shape = tensor_slab.shape
    parties = lax.axis_size("partner")
    me = lax.axis_index("partner")
    rank = mode2_factor.shape[1]
    total = fibre_col.shape[0] * lax.axis_size("blk")
    scale = 1.0 / math.sqrt(rows * parties)
    signs = sign_flips.astype(F32) * scale
    chain = Chain(jnp.stack([me >> 2, me & 1, (me >> 1) & 1, (me >> 2) & 1, me >> 3]).astype(jnp.int32))
    table = jnp.asarray(hadamard(rows), jnp.bfloat16)

    last = {}

    def go(value, mask, lane, after=()):
        after = tuple(after) + ((last[lane],) if lane in last else ())
        if after:
            value, = gate(chain, (value,), after)
        last[lane] = swap(value, mask)
        return value, last[lane]

    def along_y(pieces, got, *which, after=()):
        got[0] = pieces[0]
        for m in which or (1, 2, 3):
            got[m] = go(pieces[m], 4 * m, m, after)[1]

    def ordered(got):
        return [got[m] for m in range(4)]

    col, depth, mode3 = fibre_col[None], fibre_depth[None], mode3_factor[:, None]

    def small(value, mask, after, axis="partner"):
        value, = gate(chain, (value,), (after,))
        return value, swap(value, mask, axis)

    ct, dt, at, bt, cb, db, ab, bb = ({} for _ in range(8))
    a, c = first(chain, tensor_slab, signs[:, None], table, (0, 2))
    a_other, c_other = swap(a, 1), swap(c, 1)
    d, b = first(chain, tensor_slab, signs[:, None], table, (3, 1))
    d_other, b_other = swap(d, 1), swap(b, 1)
    c = combine_split(chain, 1, c, c_other)
    along_y(c, ct)
    a0 = combine_one(chain, 1, a, a_other, 0)
    a0, a0_other = go(a0, 2, "x0")
    d = combine_split(chain, 1, d, d_other)
    b0, b1 = (combine_one(chain, 1, b, b_other, k) for k in range(2))
    moment, gram = sample(
        chain, col, depth, signs[None], mode2_factor, mode3, tensor_slab, table, 1.0 / math.sqrt(total)
    )
    moment_other = swap(moment, 1)
    along_y(d, dt, 1)
    moment = fold(chain, 1, moment, moment_other, gram)
    a1 = combine_one(chain, 1, a, a_other, 1)
    a1, a1_other = go(a1, 2, "x1")
    along_y(d, dt, 2, 3)
    c = middle(chain, ordered(ct))

    moment, moment_other = small(moment, 1, a0_other, "blk")
    along_y(c, cb, 1, 2)
    moment = add(chain, moment, moment_other, 2 * rank)
    b0, b0_other = go(b0, 2, "x0")
    along_y(c, cb, 3)
    d = middle(chain, ordered(dt))

    moment, moment_other = small(moment, 2, a1_other, "blk")
    a = combine_split_slices(chain, 2, (a0, a1), (a0_other, a1_other))
    along_y(d, db, 1, 2)
    moment = add(chain, moment, moment_other, 2 * rank)
    b1, b1_other = go(b1, 2, "x1")
    along_y(d, db, 3)
    c0, c1 = pack(chain, ordered(cb))

    moment, moment_other = small(moment, 4, b0_other, "blk")
    along_y(a, at, 1, 2)
    summed = add(chain, moment, moment_other, 2 * rank)
    c0, c0_other = go(c0, 2, "x0")
    along_y(a, at, 3)
    d0, d1 = pack(chain, ordered(db))
    inverse, moment = inverse_of(chain, summed, rank, total)

    moment, moment_other = small(moment, 2, b1_other)
    b = combine_split_slices(chain, 2, (b0, b1), (b0_other, b1_other))
    along_y(b, bt, 1, 2)
    moment = fold(chain, 2, moment, moment_other)
    c1, c1_other = go(c1, 2, "x1")
    along_y(b, bt, 3)
    a = middle(chain, ordered(at))

    moment, moment_other = small(moment, 4, c0_other)
    along_y(a, ab, 1, 2)
    moment = fold(chain, 3, moment, moment_other)
    d0, d0_other = go(d0, 2, "x0")
    along_y(a, ab, 3)
    b = middle(chain, ordered(bt))

    moment, moment_other = small(moment, 8, c1_other)
    along_y(b, bb, 1, 2)
    moment = fold(chain, 4, moment, moment_other)
    d1, d1_other = go(d1, 2, "x1")
    along_y(b, bb, 3)
    out = end_slices(chain, 2, (c0, c1), (c0_other, c1_other), 2, shape)
    factor = times_inverse(chain, moment, inverse)
    out = end_mixed(chain, ab, 0, 2, None, None, 0, 0, out, 0)
    out = end_mixed(chain, {m: bb[m] for m in (0, 1)}, 1, 2, d0, d0_other, 3, 0, out, COST)
    out = end_mixed(chain, {2: bb[2]}, 1, 2, None, None, 0, 0, out, COST)
    out = end_mixed(chain, {3: bb[3]}, 1, 2, d1, d1_other, 3, 2, out, COST)
    return (out, factor)


def solution(mesh):
    return jax.shard_map(
        shards,
        mesh=mesh,
        in_specs=(P(None, "partner", "blk"), P("partner"), P("blk", None), P(), P("blk"), P("blk")),
        out_specs=(P(None, "partner", "blk"), P("partner", None)),
        check_vma=False,
    )
```

```python
import functools
import math

import jax
import jax.numpy as jnp
import numpy as np
from jax import lax
from jax.experimental import pallas as pl
from jax.experimental.pallas import tpu as pltpu
from jax.sharding import PartitionSpec as P

ridge = 0.1
HIGH = lax.Precision.HIGHEST
F32 = jnp.float32
HBM = pl.BlockSpec(memory_space=pltpu.HBM)
COST = 400_000_000
VMEM = pl.BlockSpec(memory_space=pltpu.VMEM)
SMEM = pl.BlockSpec(memory_space=pltpu.SMEM)


def hadamard(order_len):
    table = np.ones((1, 1), np.float32)
    while table.shape[0] < order_len:
        table = np.block([[table, table], [table, -table]])
    return table


def sign_of(bit):
    return (1 - 2 * bit).astype(F32)


def y_signs(place_ref):
    low, high = sign_of(place_ref[0] & 1), sign_of(place_ref[0] >> 1)
    return [jnp.float32(1), low, high, low * high]


def struct(*shape):
    return jax.ShapeDtypeStruct(shape, F32)


class Chain:
    def __init__(self, place):
        self.place, self.mark = place, None

    def __call__(self, body, operands, in_specs, out_shapes, out_specs, aliases=None, scratch=(), grid=(), limit=12, cost=0):
        marks = () if self.mark is None else (self.mark,)
        n_in, n_out = len(operands), len(out_shapes)

        def inner(place_ref, *refs):
            outs = refs[n_in + len(marks):]
            body(place_ref, *refs[:n_in], *outs[:n_out], *outs[n_out + 1:])

        *outs, self.mark = pl.pallas_call(
            inner,
            out_shape=list(out_shapes) + [struct(8, 128)],
            grid=grid,
            in_specs=[SMEM] + list(in_specs) + [HBM] * len(marks),
            out_specs=list(out_specs) + [HBM],
            scratch_shapes=scratch,
            input_output_aliases=aliases or {},
            compiler_params=pltpu.CompilerParams(vmem_limit_bytes=limit * 2**20),
            cost_estimate=pl.CostEstimate(flops=0, bytes_accessed=cost, transcendentals=0),
        )(self.place, *operands, *marks)
        return outs


def by_rows(rows, step, work):
    def one(i, carry):
        work(pl.ds(pl.multiple_of(i * step, step), step))
        return carry

    lax.fori_loop(0, rows // step, one, 0)


def first(chain, slab, signs, table, groups):
    rows, cols = slab.shape[1:]

    def body(place_ref, signs_ref, table_ref, x_ref, *refs):
        o_refs, held, sems = refs[:2], refs[2], refs[3]
        copies = [
            pltpu.make_async_copy(x_ref.at[2 * group + i], held.at[2 * n + i], sems.at[2 * n + i])
            for n, group in enumerate(groups) for i in range(2)
        ]
        for copy in copies:
            copy.start()
        for n, copy in enumerate(copies):
            copy.wait()
            value = held[n] * signs_ref[...]
            high = value.astype(jnp.bfloat16)
            low = (value - high.astype(F32)).astype(jnp.bfloat16)
            o_refs[n // 2][n % 2] = jnp.dot(table_ref[...], high, preferred_element_type=F32) + jnp.dot(
                table_ref[...], low, preferred_element_type=F32
            )

    return chain(
        body, (signs, table, slab), [VMEM, VMEM, HBM], [struct(2, rows, cols)] * 2, [VMEM] * 2,
        scratch=[pltpu.VMEM((4, rows, cols), F32), pltpu.SemaphoreType.DMA((4,))], limit=48,
    )


def combine_under(chain, which, own, other, k, more, rank):
    rows, cols = own.shape[1:]

    def body(place_ref, a_ref, b_ref, more_ref, o_ref):
        sign = sign_of(place_ref[which])

        def work(at):
            o_ref[at, :] = b_ref[k, at, :] + a_ref[k, at, :] * sign

        by_rows(rows, 64, work)
        o_ref[rows:] = more_ref[:rank]

    return chain(body, (own, other, more), [VMEM] * 3, [struct(rows + rank, cols)], [VMEM])[0]


def combine_split(chain, which, own, other):
    rows, cols = own.shape[1:]
    half = rows // 2

    def body(place_ref, a_ref, b_ref, *o_refs):
        sign = sign_of(place_ref[which])
        for m in range(4):
            piece = place_ref[0] ^ m
            a, b = (ref.at[piece >> 1, pl.ds(pl.multiple_of((piece & 1) * half, half), half)] for ref in (a_ref, b_ref))

            def work(at, a=a, b=b, o=o_refs[m]):
                o[at, :] = b[at, :] + a[at, :] * sign

            by_rows(half, 64, work)

    return chain(body, (own, other), [VMEM] * 2, [struct(half, cols)] * 4, [VMEM] * 4)


def combine_one(chain, which, own, other, k):
    rows, cols = own.shape[1:]

    def body(place_ref, a_ref, b_ref, o_ref):
        sign = sign_of(place_ref[which])

        def work(at):
            o_ref[at, :] = b_ref[k, at, :] + a_ref[k, at, :] * sign

        by_rows(rows, 64, work)

    return chain(body, (own, other), [VMEM] * 2, [struct(rows, cols)], [VMEM])[0]


def combine_split_slices(chain, which, own, other):
    rows, cols = own[0].shape
    half, extra = rows // 2, (own[1].shape[0] - rows) // 4

    def body(place_ref, *refs):
        sign = sign_of(place_ref[which])
        for m in range(4):
            piece = place_ref[0] ^ m
            for k in range(2):
                @pl.when(piece >> 1 == k)
                def _(m=m, k=k, piece=piece):
                    a, b = (ref.at[pl.ds(pl.multiple_of((piece & 1) * half, half), half)] for ref in (refs[k], refs[2 + k]))

                    def work(at):
                        refs[4 + m][at, :] = b[at, :] + a[at, :] * sign

                    by_rows(half, 64, work)

            if extra:
                at = pl.ds(pl.multiple_of(rows + piece * extra, extra), extra)
                refs[4 + m][half:] = refs[3][at, :] + refs[1][at, :] * sign

    return chain(
        body, tuple(own) + tuple(other), [VMEM] * 4, [struct(half + extra, cols)] * 4, [VMEM] * 4
    )


def middle(chain, parts):
    half, cols = parts[0].shape

    def body(place_ref, *refs):
        signs = y_signs(place_ref)

        def work(at):
            a, b, c, d = (refs[m][at, :] * signs[m] for m in range(4))
            s, t, u, v = a + b, a - b, c + d, c - d
            for m, value in enumerate((s + u, t + v, s - u, t - v)):
                refs[4 + m][at, :] = value * (signs[3] * signs[m])

        by_rows(half, 16, work)

    return chain(body, tuple(parts), [VMEM] * 4, [struct(half, cols)] * 4, [VMEM] * 4)


def pack(chain, parts):
    half, cols = parts[0].shape

    def body(place_ref, *refs):
        for m in range(4):
            def work(at, m=m):
                refs[4 + m // 2][m % 2, at, :] = refs[m][at, :]

            by_rows(half, 64, work)

    return chain(body, tuple(parts), [VMEM] * 4, [struct(2, half, cols)] * 2, [VMEM] * 2)


def gate(chain, values, after):
    n = len(values)

    def body(place_ref, *refs):
        for i in range(n):
            flat = refs[i].shape[0] if len(refs[i].shape) == 2 else None

            def work(at, i=i):
                refs[n + len(after) + i][at] = refs[i][at]

            if flat:
                by_rows(flat, 16, work)
            else:
                by_rows(refs[i].shape[0], 1, work)

    return chain(
        body, tuple(values) + tuple(after), [VMEM] * (n + len(after)), [struct(*v.shape) for v in values], [VMEM] * n
    )


def to_place(place_ref, source, out, group, m, half, sem):
    piece = place_ref[0] ^ m
    start = pl.multiple_of((piece & 1) * half, half)
    copy = pltpu.make_async_copy(source, out.at[2 * group + (piece >> 1), pl.ds(start, half), :], sem)
    copy.start()
    return copy


def end_slices(chain, which, own, other, group, shape):
    half, cols = own[0].shape[1:]

    def body(place_ref, *refs):
        out, held, sems = refs[4:]
        sign = sign_of(place_ref[which])
        copies = []
        for m in range(4):
            def work(at, m=m):
                held[m, at, :] = refs[2 + m // 2][m % 2, at, :] + refs[m // 2][m % 2, at, :] * sign

            by_rows(half, 64, work)
            copies.append(to_place(place_ref, held.at[m], out, group, m, half, sems.at[m]))
        for copy in copies:
            copy.wait()

    return chain(
        body, tuple(own) + tuple(other), [VMEM] * 4, [struct(*shape)], [HBM],
        scratch=[pltpu.VMEM((4, half, cols), F32), pltpu.SemaphoreType.DMA((4,))],
    )[0]


def end_mixed(chain, parts, group, which, own, other, other_group, first_piece, buffer, cost=0):
    half, cols = buffer.shape[1] // 2, buffer.shape[2]
    names = list(parts)
    n, pieces = len(names), 0 if own is None else own.shape[0]
    pair = () if own is None else (own, other)

    def body(place_ref, *refs):
        out, held, sems = refs[n + len(pair) + 1:]
        copies = [
            to_place(place_ref, refs[i].at[pl.ds(0, half)], out, group, m, half, sems.at[i])
            for i, m in enumerate(names)
        ]
        for m in range(pieces):
            def work(at, m=m):
                held[m, at, :] = refs[n + 1][m, at, :] + refs[n][m, at, :] * sign_of(place_ref[which])

            by_rows(half, 64, work)
            copies.append(to_place(place_ref, held.at[m], out, other_group, first_piece + m, half, sems.at[n + m]))
        for copy in copies:
            copy.wait()

    return chain(
        body, tuple(parts[m] for m in names) + pair + (buffer,), [VMEM] * (n + len(pair)) + [HBM],
        [struct(*buffer.shape)], [HBM], aliases={n + len(pair) + 1: 0}, cost=cost,
        scratch=[pltpu.VMEM((max(pieces, 1), half, cols), F32), pltpu.SemaphoreType.DMA((n + pieces,))],
    )[0]


def times_inverse(chain, parts, half, inverse):
    extra, cols = parts[0].shape[0] - half, parts[0].shape[1]

    def body(place_ref, *refs):
        inverse_ref, o_ref, moment = refs[4:]
        for m in range(4):
            start = pl.multiple_of((place_ref[0] ^ m) * extra, extra)
            moment[pl.ds(start, extra), :] = refs[m][half:]
        o_ref[...] = lax.dot_general(
            moment[...], inverse_ref[...], (((0,), (0,)), ((), ())), precision=HIGH, preferred_element_type=F32
        )

    return chain(
        body, tuple(parts) + (inverse,), [VMEM] * 5, [struct(cols, inverse.shape[0])], [VMEM],
        scratch=[pltpu.VMEM((4 * extra, cols), F32)],
    )[0]


def in_three(value):
    high = value.astype(jnp.bfloat16)
    rest = value - high.astype(F32)
    middle_part = rest.astype(jnp.bfloat16)
    return high, middle_part, (rest - middle_part.astype(F32)).astype(jnp.bfloat16)


def sample(chain, col, depth, signs, mode2, mode3, slab, table, factor):
    slices, rows, cols = slab.shape
    rank = mode2.shape[1]
    dot = functools.partial(jnp.dot, preferred_element_type=F32)

    def body(place_ref, col_ref, depth_ref, signs_ref, mode2_ref, mode3_ref, table_ref, x_ref, o_ref, total, gram, held, sems):
        copies = [pltpu.make_async_copy(x_ref.at[k], held.at[k], sems.at[k]) for k in range(slices)]
        for copy in copies:
            copy.start()
        total[...] = jnp.zeros((rows, rank), F32)
        gram[...] = jnp.zeros((rank, rank), F32)

        for k, copy in enumerate(copies):
            khatri = mode2_ref[...] * mode3_ref[k]
            weighted = khatri * counts(col_ref, depth_ref, k, cols)
            gram[...] += lax.dot_general(
                khatri, weighted, (((0,), (0,)), ((), ())), precision=HIGH, preferred_element_type=F32
            )
            copy.wait()
            weights = jnp.concatenate(in_three(weighted), axis=1)
            x_high, x_middle, x_low = in_three(held[k])
            most = dot(x_high, weights)
            some = dot(x_middle, weights[:, : 2 * rank])
            total[...] += (
                (dot(x_low, weights[:, :rank]) + some[:, rank:] + most[:, 2 * rank :])
                + (some[:, :rank] + most[:, rank : 2 * rank])
                + most[:, :rank]
            )

        part = total[...].T * (signs_ref[...] * factor)
        done = jnp.zeros((rank, rows), F32)
        for piece in in_three(part):
            done = done + dot(piece, table_ref[...])
        o_ref[:rank] = done
        square = gram[...]
        lines = rank * rank // rows
        o_ref[rank:] = jnp.concatenate([square[q : q + lines] for q in range(0, rank, lines)], axis=1)

    return chain(
        body, (col, depth, signs, mode2, mode3, table, slab), [VMEM] * 6 + [HBM], [struct(rank + rank * rank // rows, rows)], [VMEM],
        scratch=[
            pltpu.VMEM((rows, rank), F32), pltpu.VMEM((rank, rank), F32),
            pltpu.VMEM((slices, rows, cols), F32), pltpu.SemaphoreType.DMA((slices,)),
        ],
        limit=48,
    )[0]


def counts(col_ref, depth_ref, k, cols):
    chosen = jnp.where(depth_ref[...] == k, col_ref[...], -1)
    hits = lax.broadcasted_iota(jnp.int32, (cols, chosen.shape[1]), 0) == chosen
    return jnp.sum(hits.astype(F32), axis=1, keepdims=True)


def fold(chain, which, own, other, rows):
    def body(place_ref, a_ref, b_ref, o_ref):
        o_ref[...] = a_ref[...]
        o_ref[:rows] = b_ref[:rows] + a_ref[:rows] * sign_of(place_ref[which])

    return chain(body, (own, other), [VMEM] * 2, [struct(*own.shape)], [VMEM])[0]


def add(chain, own, other, rows):
    def body(place_ref, a_ref, b_ref, o_ref):
        o_ref[...] = a_ref[:rows] + b_ref[:rows]

    return chain(body, (own, other), [VMEM] * 2, [struct(rows, own.shape[1])], [VMEM])[0]


def inverse_of(chain, summed, rank, total):
    def body(place_ref, x_ref, o_ref, work):
        row = lax.broadcasted_iota(jnp.int32, (rank, 2 * rank), 0)
        col = lax.broadcasted_iota(jnp.int32, (rank, 2 * rank), 1)
        square_row, square_col = row[:, :rank], col[:, :rank]
        eye = jnp.where(square_row == square_col, 1.0, 0.0)
        packed = x_ref[rank:]
        lines = packed.shape[0]
        gram = jnp.concatenate([packed[:, i * rank : (i + 1) * rank] for i in range(rank // lines)], axis=0)
        gram = gram * (1.0 / total) + ridge * eye
        work[:, :rank] = gram
        work[:, rank:] = eye

        def step(j, carry):
            now = work[...]
            pivot_row = work[pl.ds(j, 1), :]
            pivot = jnp.sum(jnp.where(col[:1] == j, pivot_row, 0.0), axis=1, keepdims=True)
            pivot_row = pivot_row / pivot
            column = jnp.sum(jnp.where(col == j, now, 0.0), axis=1, keepdims=True)
            work[...] = jnp.where(row == j, pivot_row, now - column * pivot_row)
            return carry

        lax.fori_loop(0, rank, step, 0)
        found = work[:, rank:]
        dot = lambda a, b: jnp.dot(a, b, precision=HIGH, preferred_element_type=F32)
        o_ref[...] = found + dot(found, eye - dot(gram, found))

    return chain(
        body, (summed,), [VMEM], [struct(rank, rank)], [VMEM], scratch=[pltpu.VMEM((rank, 2 * rank), F32)],
    )[0]


def swap(value, mask, axis="partner"):
    return lax.ppermute(value, axis, [(s, s ^ mask) for s in range(lax.axis_size(axis))])


def shards(tensor_slab, sign_flips, mode2_factor, mode3_factor, fibre_col, fibre_depth):
    slices, rows, cols = shape = tensor_slab.shape
    parties = lax.axis_size("partner")
    me = lax.axis_index("partner")
    rank = mode2_factor.shape[1]
    total = fibre_col.shape[0] * lax.axis_size("blk")
    scale = 1.0 / math.sqrt(rows * parties)
    signs = sign_flips.astype(F32) * scale
    chain = Chain(jnp.stack([me >> 2, me & 1, (me >> 1) & 1, (me >> 2) & 1, me >> 3]).astype(jnp.int32))
    table = jnp.asarray(hadamard(rows), jnp.bfloat16)

    last = {}

    def go(value, mask, lane, after=()):
        after = tuple(after) + ((last[lane],) if lane in last else ())
        if after:
            value, = gate(chain, (value,), after)
        last[lane] = swap(value, mask)
        return value, last[lane]

    def along_y(pieces, got, *which, after=()):
        got[0] = pieces[0]
        for m in which or (1, 2, 3):
            got[m] = go(pieces[m], 4 * m, m, after)[1]

    def ordered(got):
        return [got[m] for m in range(4)]

    col, depth, mode3 = fibre_col[None], fibre_depth[None], mode3_factor[:, None]

    summed = sample(
        chain, col, depth, signs[None], mode2_factor, mode3, tensor_slab, table, 1.0 / math.sqrt(total)
    )
    summed_other = swap(summed, 1)
    a, c = first(chain, tensor_slab, signs[:, None], table, (0, 2))
    a_other, c_other = swap(a, 1), swap(c, 1)
    summed = fold(chain, 1, summed, summed_other, rank)
    summed_other = swap(summed, 1, "blk")
    d, b = first(chain, tensor_slab, signs[:, None], table, (3, 1))
    d_other, b_other = swap(d, 1), swap(b, 1)
    summed = add(chain, summed, summed_other, summed.shape[0])
    summed_other = swap(summed, 2, "blk")

    ct, dt, at, bt, cb, db, ab, bb = ({} for _ in range(8))
    c = combine_split(chain, 1, c, c_other)
    along_y(c, ct)
    a0 = combine_one(chain, 1, a, a_other, 0)
    a0, a0_other = go(a0, 2, "x0")
    summed = add(chain, summed, summed_other, summed.shape[0])
    summed_other = swap(summed, 4, "blk")
    a1 = combine_one(chain, 1, a, a_other, 1)
    d = combine_split(chain, 1, d, d_other)
    b0 = combine_one(chain, 1, b, b_other, 0)
    summed = add(chain, summed, summed_other, summed.shape[0])
    a1, a1_other = go(gate(chain, (a1,), (summed,))[0], 2, "x1")
    b1 = combine_under(chain, 1, b, b_other, 1, summed, rank)
    along_y(d, dt)
    c = middle(chain, ordered(ct))
    b0, b0_other = go(b0, 2, "x0")
    b1, b1_other = go(b1, 2, "x1")
    along_y(c, cb)
    d = middle(chain, ordered(dt))
    a = combine_split_slices(chain, 2, (a0, a1), (a0_other, a1_other))
    along_y(d, db)
    c0, c1 = pack(chain, ordered(cb))
    c0, c0_other = go(c0, 2, "x0")
    c1, c1_other = go(c1, 2, "x1")
    along_y(a, at)
    d0, d1 = pack(chain, ordered(db))
    b = combine_split_slices(chain, 2, (b0, b1), (b0_other, b1_other))
    along_y(b, bt, 1)
    inverse = inverse_of(chain, summed, rank, total)
    along_y(b, bt, 2, 3)
    a = middle(chain, ordered(at))
    d0, d0_other = go(d0, 2, "x0")
    d1, d1_other = go(d1, 2, "x1")
    along_y(a, ab)
    b = middle(chain, ordered(bt))
    along_y(b, bb)
    out = end_slices(chain, 2, (c0, c1), (c0_other, c1_other), 2, shape)
    out = end_mixed(chain, ab, 0, 2, None, None, 0, 0, out)
    out = end_mixed(chain, {m: bb[m] for m in (0, 1)}, 1, 2, d0, d0_other, 3, 0, out, COST)
    out = end_mixed(chain, {2: bb[2]}, 1, 2, None, None, 0, 0, out, COST)
    out = end_mixed(chain, {3: bb[3]}, 1, 2, d1, d1_other, 3, 2, out, COST)
    factor = times_inverse(chain, ordered(bb), rows // 2, inverse)
    return (out, factor)


def solution(mesh):
    return jax.shard_map(
        shards,
        mesh=mesh,
        in_specs=(P(None, "partner", "blk"), P("partner"), P("blk", None), P(), P("blk"), P("blk")),
        out_specs=(P(None, "partner", "blk"), P("partner", None)),
        check_vma=False,
    )
```

```python
import functools
import math

import jax
import jax.numpy as jnp
import numpy as np
from jax import lax
from jax.experimental import pallas as pl
from jax.experimental.pallas import tpu as pltpu
from jax.sharding import PartitionSpec as P

ridge = 0.1
HIGH = lax.Precision.HIGHEST
F32 = jnp.float32
HBM = pl.BlockSpec(memory_space=pltpu.HBM)
COST = 400_000_000
VMEM = pl.BlockSpec(memory_space=pltpu.VMEM)
SMEM = pl.BlockSpec(memory_space=pltpu.SMEM)


def hadamard(order_len):
    table = np.ones((1, 1), np.float32)
    while table.shape[0] < order_len:
        table = np.block([[table, table], [table, -table]])
    return table


def sign_of(bit):
    return (1 - 2 * bit).astype(F32)


def y_signs(place_ref):
    low, high = sign_of(place_ref[0] & 1), sign_of(place_ref[0] >> 1)
    return [jnp.float32(1), low, high, low * high]


def struct(*shape):
    return jax.ShapeDtypeStruct(shape, F32)


class Chain:
    def __init__(self, place):
        self.place, self.mark = place, None

    def __call__(self, body, operands, in_specs, out_shapes, out_specs, aliases=None, scratch=(), grid=(), limit=12, cost=0):
        marks = () if self.mark is None else (self.mark,)
        n_in, n_out = len(operands), len(out_shapes)

        def inner(place_ref, *refs):
            outs = refs[n_in + len(marks):]
            body(place_ref, *refs[:n_in], *outs[:n_out], *outs[n_out + 1:])

        *outs, self.mark = pl.pallas_call(
            inner,
            out_shape=list(out_shapes) + [struct(8, 128)],
            grid=grid,
            in_specs=[SMEM] + list(in_specs) + [HBM] * len(marks),
            out_specs=list(out_specs) + [HBM],
            scratch_shapes=scratch,
            input_output_aliases=aliases or {},
            compiler_params=pltpu.CompilerParams(vmem_limit_bytes=limit * 2**20),
            cost_estimate=pl.CostEstimate(flops=0, bytes_accessed=cost, transcendentals=0),
        )(self.place, *operands, *marks)
        return outs


def by_rows(rows, step, work):
    def one(i, carry):
        work(pl.ds(pl.multiple_of(i * step, step), step))
        return carry

    lax.fori_loop(0, rows // step, one, 0)


def first(chain, slab, signs, table, groups):
    rows, cols = slab.shape[1:]

    def body(place_ref, signs_ref, table_ref, x_ref, *refs):
        o_refs, held, sems = refs[:2], refs[2], refs[3]
        copies = [
            pltpu.make_async_copy(x_ref.at[2 * group + i], held.at[2 * n + i], sems.at[2 * n + i])
            for n, group in enumerate(groups) for i in range(2)
        ]
        for copy in copies:
            copy.start()
        for n, copy in enumerate(copies):
            copy.wait()
            value = held[n] * signs_ref[...]
            high = value.astype(jnp.bfloat16)
            low = (value - high.astype(F32)).astype(jnp.bfloat16)
            o_refs[n // 2][n % 2] = jnp.dot(table_ref[...], high, preferred_element_type=F32) + jnp.dot(
                table_ref[...], low, preferred_element_type=F32
            )

    return chain(
        body, (signs, table, slab), [VMEM, VMEM, HBM], [struct(2, rows, cols)] * 2, [VMEM] * 2,
        scratch=[pltpu.VMEM((4, rows, cols), F32), pltpu.SemaphoreType.DMA((4,))], limit=48,
    )


def combine_under(chain, which, own, other, k, more, rank):
    rows, cols = own.shape[1:]

    def body(place_ref, a_ref, b_ref, more_ref, o_ref):
        sign = sign_of(place_ref[which])

        def work(at):
            o_ref[at, :] = b_ref[k, at, :] + a_ref[k, at, :] * sign

        by_rows(rows, 64, work)
        o_ref[rows:] = more_ref[:rank]

    return chain(body, (own, other, more), [VMEM] * 3, [struct(rows + rank, cols)], [VMEM])[0]


def combine_split(chain, which, own, other):
    rows, cols = own.shape[1:]
    half = rows // 2

    def body(place_ref, a_ref, b_ref, *o_refs):
        sign = sign_of(place_ref[which])
        for m in range(4):
            piece = place_ref[0] ^ m
            a, b = (ref.at[piece >> 1, pl.ds(pl.multiple_of((piece & 1) * half, half), half)] for ref in (a_ref, b_ref))

            def work(at, a=a, b=b, o=o_refs[m]):
                o[at, :] = b[at, :] + a[at, :] * sign

            by_rows(half, 64, work)

    return chain(body, (own, other), [VMEM] * 2, [struct(half, cols)] * 4, [VMEM] * 4)


def combine_one(chain, which, own, other, k):
    rows, cols = own.shape[1:]

    def body(place_ref, a_ref, b_ref, o_ref):
        sign = sign_of(place_ref[which])

        def work(at):
            o_ref[at, :] = b_ref[k, at, :] + a_ref[k, at, :] * sign

        by_rows(rows, 64, work)

    return chain(body, (own, other), [VMEM] * 2, [struct(rows, cols)], [VMEM])[0]


def combine_split_slices(chain, which, own, other):
    rows, cols = own[0].shape
    half, extra = rows // 2, (own[1].shape[0] - rows) // 4

    def body(place_ref, *refs):
        sign = sign_of(place_ref[which])
        for m in range(4):
            piece = place_ref[0] ^ m
            for k in range(2):
                @pl.when(piece >> 1 == k)
                def _(m=m, k=k, piece=piece):
                    a, b = (ref.at[pl.ds(pl.multiple_of((piece & 1) * half, half), half)] for ref in (refs[k], refs[2 + k]))

                    def work(at):
                        refs[4 + m][at, :] = b[at, :] + a[at, :] * sign

                    by_rows(half, 64, work)

            if extra:
                at = pl.ds(pl.multiple_of(rows + piece * extra, extra), extra)
                refs[4 + m][half:] = refs[3][at, :] + refs[1][at, :] * sign

    return chain(
        body, tuple(own) + tuple(other), [VMEM] * 4, [struct(half + extra, cols)] * 4, [VMEM] * 4
    )


def middle(chain, parts):
    half, cols = parts[0].shape

    def body(place_ref, *refs):
        signs = y_signs(place_ref)

        def work(at):
            a, b, c, d = (refs[m][at, :] * signs[m] for m in range(4))
            s, t, u, v = a + b, a - b, c + d, c - d
            for m, value in enumerate((s + u, t + v, s - u, t - v)):
                refs[4 + m][at, :] = value * (signs[3] * signs[m])

        by_rows(half, 16, work)

    return chain(body, tuple(parts), [VMEM] * 4, [struct(half, cols)] * 4, [VMEM] * 4)


def pack(chain, parts):
    half, cols = parts[0].shape

    def body(place_ref, *refs):
        for m in range(4):
            def work(at, m=m):
                refs[4 + m // 2][m % 2, at, :] = refs[m][at, :]

            by_rows(half, 64, work)

    return chain(body, tuple(parts), [VMEM] * 4, [struct(2, half, cols)] * 2, [VMEM] * 2)


def gate(chain, values, after):
    n = len(values)

    def body(place_ref, *refs):
        for i in range(n):
            flat = refs[i].shape[0] if len(refs[i].shape) == 2 else None

            def work(at, i=i):
                refs[n + len(after) + i][at] = refs[i][at]

            if flat:
                by_rows(flat, 16, work)
            else:
                by_rows(refs[i].shape[0], 1, work)

    return chain(
        body, tuple(values) + tuple(after), [VMEM] * (n + len(after)), [struct(*v.shape) for v in values], [VMEM] * n
    )


def to_place(place_ref, source, out, group, m, half, sem):
    piece = place_ref[0] ^ m
    start = pl.multiple_of((piece & 1) * half, half)
    copy = pltpu.make_async_copy(source, out.at[2 * group + (piece >> 1), pl.ds(start, half), :], sem)
    copy.start()
    return copy


def end_slices(chain, which, own, other, group, shape):
    half, cols = own[0].shape[1:]

    def body(place_ref, *refs):
        out, held, sems = refs[4:]
        sign = sign_of(place_ref[which])
        copies = []
        for m in range(4):
            def work(at, m=m):
                held[m, at, :] = refs[2 + m // 2][m % 2, at, :] + refs[m // 2][m % 2, at, :] * sign

            by_rows(half, 64, work)
            copies.append(to_place(place_ref, held.at[m], out, group, m, half, sems.at[m]))
        for copy in copies:
            copy.wait()

    return chain(
        body, tuple(own) + tuple(other), [VMEM] * 4, [struct(*shape)], [HBM],
        scratch=[pltpu.VMEM((4, half, cols), F32), pltpu.SemaphoreType.DMA((4,))],
    )[0]


def end_mixed(chain, parts, group, which, own, other, other_group, first_piece, buffer, cost=0):
    half, cols = buffer.shape[1] // 2, buffer.shape[2]
    names = list(parts)
    n, pieces = len(names), 0 if own is None else own.shape[0]
    pair = () if own is None else (own, other)

    def body(place_ref, *refs):
        out, held, sems = refs[n + len(pair) + 1:]
        copies = [
            to_place(place_ref, refs[i].at[pl.ds(0, half)], out, group, m, half, sems.at[i])
            for i, m in enumerate(names)
        ]
        for m in range(pieces):
            def work(at, m=m):
                held[m, at, :] = refs[n + 1][m, at, :] + refs[n][m, at, :] * sign_of(place_ref[which])

            by_rows(half, 64, work)
            copies.append(to_place(place_ref, held.at[m], out, other_group, first_piece + m, half, sems.at[n + m]))
        for copy in copies:
            copy.wait()

    return chain(
        body, tuple(parts[m] for m in names) + pair + (buffer,), [VMEM] * (n + len(pair)) + [HBM],
        [struct(*buffer.shape)], [HBM], aliases={n + len(pair) + 1: 0}, cost=cost,
        scratch=[pltpu.VMEM((max(pieces, 1), half, cols), F32), pltpu.SemaphoreType.DMA((n + pieces,))],
    )[0]


def times_inverse(chain, parts, half, inverse):
    extra, cols = parts[0].shape[0] - half, parts[0].shape[1]

    def body(place_ref, *refs):
        inverse_ref, o_ref, moment = refs[4:]
        for m in range(4):
            start = pl.multiple_of((place_ref[0] ^ m) * extra, extra)
            moment[pl.ds(start, extra), :] = refs[m][half:]
        o_ref[...] = lax.dot_general(
            moment[...], inverse_ref[...], (((0,), (0,)), ((), ())), precision=HIGH, preferred_element_type=F32
        )

    return chain(
        body, tuple(parts) + (inverse,), [VMEM] * 5, [struct(cols, inverse.shape[0])], [VMEM],
        scratch=[pltpu.VMEM((4 * extra, cols), F32)],
    )[0]


def in_three(value):
    high = value.astype(jnp.bfloat16)
    rest = value - high.astype(F32)
    middle_part = rest.astype(jnp.bfloat16)
    return high, middle_part, (rest - middle_part.astype(F32)).astype(jnp.bfloat16)


def sample(chain, col, depth, signs, mode2, mode3, slab, table, factor):
    slices, rows, cols = slab.shape
    rank = mode2.shape[1]
    dot = functools.partial(jnp.dot, preferred_element_type=F32)

    def body(place_ref, col_ref, depth_ref, signs_ref, mode2_ref, mode3_ref, turn_ref, table_ref, x_ref, o_ref, total, held, sems):
        copies = [pltpu.make_async_copy(x_ref.at[k], held.at[k], sems.at[k]) for k in range(slices)]
        for copy in copies:
            copy.start()
        total[...] = jnp.zeros((rows + rank, rank), F32)
        turned = mode2_ref[...].T

        for k, copy in enumerate(copies):
            khatri = mode2_ref[...] * mode3_ref[k]
            weighted = khatri * counts(col_ref, depth_ref, k, cols)
            copy.wait()
            weights = jnp.concatenate(in_three(weighted), axis=1)
            x_high, x_middle, x_low = in_three(jnp.concatenate([held[k], turned * turn_ref[k]], axis=0))
            most = dot(x_high, weights)
            some = dot(x_middle, weights[:, : 2 * rank])
            total[...] += (
                (dot(x_low, weights[:, :rank]) + some[:, rank:] + most[:, 2 * rank :])
                + (some[:, :rank] + most[:, rank : 2 * rank])
                + most[:, :rank]
            )

        part = total[:rows].T * (signs_ref[...] * factor)
        done = jnp.zeros((rank, rows), F32)
        for piece in in_three(part):
            done = done + dot(piece, table_ref[...])
        o_ref[:rank] = done
        square = total[rows:]
        lines = rank * rank // rows
        o_ref[rank:] = jnp.concatenate([square[q : q + lines] for q in range(0, rank, lines)], axis=1)

    return chain(
        body, (col, depth, signs, mode2, mode3, mode3[:, 0, :, None], table, slab), [VMEM] * 7 + [HBM], [struct(rank + rank * rank // rows, rows)], [VMEM],
        scratch=[
            pltpu.VMEM((rows + rank, rank), F32),
            pltpu.VMEM((slices, rows, cols), F32), pltpu.SemaphoreType.DMA((slices,)),
        ],
        limit=48,
    )[0]


def counts(col_ref, depth_ref, k, cols):
    chosen = jnp.where(depth_ref[...] == k, col_ref[...], -1)
    hits = lax.broadcasted_iota(jnp.int32, (cols, chosen.shape[1]), 0) == chosen
    return jnp.sum(hits.astype(F32), axis=1, keepdims=True)


def fold(chain, which, own, other, rows):
    def body(place_ref, a_ref, b_ref, o_ref):
        o_ref[...] = a_ref[...]
        o_ref[:rows] = b_ref[:rows] + a_ref[:rows] * sign_of(place_ref[which])

    return chain(body, (own, other), [VMEM] * 2, [struct(*own.shape)], [VMEM])[0]


def add(chain, own, other, rows):
    def body(place_ref, a_ref, b_ref, o_ref):
        o_ref[...] = a_ref[:rows] + b_ref[:rows]

    return chain(body, (own, other), [VMEM] * 2, [struct(rows, own.shape[1])], [VMEM])[0]


def inverse_of(chain, summed, rank, total):
    def body(place_ref, x_ref, o_ref, work):
        row = lax.broadcasted_iota(jnp.int32, (rank, 2 * rank), 0)
        col = lax.broadcasted_iota(jnp.int32, (rank, 2 * rank), 1)
        square_row, square_col = row[:, :rank], col[:, :rank]
        eye = jnp.where(square_row == square_col, 1.0, 0.0)
        packed = x_ref[rank:]
        lines = packed.shape[0]
        gram = jnp.concatenate([packed[:, i * rank : (i + 1) * rank] for i in range(rank // lines)], axis=0)
        gram = gram * (1.0 / total) + ridge * eye
        work[:, :rank] = gram
        work[:, rank:] = eye

        def step(j, carry):
            now = work[...]
            pivot_row = work[pl.ds(j, 1), :]
            pivot = jnp.sum(jnp.where(col[:1] == j, pivot_row, 0.0), axis=1, keepdims=True)
            pivot_row = pivot_row / pivot
            column = jnp.sum(jnp.where(col == j, now, 0.0), axis=1, keepdims=True)
            work[...] = jnp.where(row == j, pivot_row, now - column * pivot_row)
            return carry

        lax.fori_loop(0, rank, step, 0)
        found = work[:, rank:]
        dot = lambda a, b: jnp.dot(a, b, precision=HIGH, preferred_element_type=F32)
        o_ref[...] = found + dot(found, eye - dot(gram, found))

    return chain(
        body, (summed,), [VMEM], [struct(rank, rank)], [VMEM], scratch=[pltpu.VMEM((rank, 2 * rank), F32)],
    )[0]


def swap(value, mask, axis="partner"):
    return lax.ppermute(value, axis, [(s, s ^ mask) for s in range(lax.axis_size(axis))])


def shards(tensor_slab, sign_flips, mode2_factor, mode3_factor, fibre_col, fibre_depth):
    slices, rows, cols = shape = tensor_slab.shape
    parties = lax.axis_size("partner")
    me = lax.axis_index("partner")
    rank = mode2_factor.shape[1]
    total = fibre_col.shape[0] * lax.axis_size("blk")
    scale = 1.0 / math.sqrt(rows * parties)
    signs = sign_flips.astype(F32) * scale
    chain = Chain(jnp.stack([me >> 2, me & 1, (me >> 1) & 1, (me >> 2) & 1, me >> 3]).astype(jnp.int32))
    table = jnp.asarray(hadamard(rows), jnp.bfloat16)

    last = {}

    def go(value, mask, lane, after=()):
        after = tuple(after) + ((last[lane],) if lane in last else ())
        if after:
            value, = gate(chain, (value,), after)
        last[lane] = swap(value, mask)
        return value, last[lane]

    def along_y(pieces, got, *which, after=()):
        got[0] = pieces[0]
        for m in which or (1, 2, 3):
            got[m] = go(pieces[m], 4 * m, m, after)[1]

    def ordered(got):
        return [got[m] for m in range(4)]

    col, depth, mode3 = fibre_col[None], fibre_depth[None], mode3_factor[:, None]

    summed = sample(
        chain, col, depth, signs[None], mode2_factor, mode3, tensor_slab, table, 1.0 / math.sqrt(total)
    )
    summed_other = swap(summed, 1)
    a, c = first(chain, tensor_slab, signs[:, None], table, (0, 2))
    a_other, c_other = swap(a, 1), swap(c, 1)
    summed = fold(chain, 1, summed, summed_other, rank)
    summed_other = swap(summed, 1, "blk")
    d, b = first(chain, tensor_slab, signs[:, None], table, (3, 1))
    d_other, b_other = swap(d, 1), swap(b, 1)
    summed = add(chain, summed, summed_other, summed.shape[0])
    summed_other = swap(summed, 2, "blk")

    ct, dt, at, bt, cb, db, ab, bb = ({} for _ in range(8))
    c = combine_split(chain, 1, c, c_other)
    along_y(c, ct)
    a0 = combine_one(chain, 1, a, a_other, 0)
    a0, a0_other = go(a0, 2, "x0")
    summed = add(chain, summed, summed_other, summed.shape[0])
    summed_other = swap(summed, 4, "blk")
    a1 = combine_one(chain, 1, a, a_other, 1)
    d = combine_split(chain, 1, d, d_other)
    b0 = combine_one(chain, 1, b, b_other, 0)
    summed = add(chain, summed, summed_other, summed.shape[0])
    a1, a1_other = go(gate(chain, (a1,), (summed,))[0], 2, "x1")
    b1 = combine_under(chain, 1, b, b_other, 1, summed, rank)
    along_y(d, dt)
    c = middle(chain, ordered(ct))
    b0, b0_other = go(b0, 2, "x0")
    b1, b1_other = go(b1, 2, "x1")
    along_y(c, cb)
    d = middle(chain, ordered(dt))
    a = combine_split_slices(chain, 2, (a0, a1), (a0_other, a1_other))
    along_y(d, db)
    c0, c1 = pack(chain, ordered(cb))
    c0, c0_other = go(c0, 2, "x0")
    c1, c1_other = go(c1, 2, "x1")
    along_y(a, at)
    d0, d1 = pack(chain, ordered(db))
    b = combine_split_slices(chain, 2, (b0, b1), (b0_other, b1_other))
    along_y(b, bt, 1)
    inverse = inverse_of(chain, summed, rank, total)
    along_y(b, bt, 2, 3)
    a = middle(chain, ordered(at))
    d0, d0_other = go(d0, 2, "x0")
    d1, d1_other = go(d1, 2, "x1")
    along_y(a, ab)
    b = middle(chain, ordered(bt))
    along_y(b, bb)
    out = end_slices(chain, 2, (c0, c1), (c0_other, c1_other), 2, shape)
    out = end_mixed(chain, ab, 0, 2, None, None, 0, 0, out)
    out = end_mixed(chain, {m: bb[m] for m in (0, 1)}, 1, 2, d0, d0_other, 3, 0, out, COST)
    out = end_mixed(chain, {2: bb[2]}, 1, 2, None, None, 0, 0, out, COST)
    out = end_mixed(chain, {3: bb[3]}, 1, 2, d1, d1_other, 3, 2, out, COST)
    factor = times_inverse(chain, ordered(bb), rows // 2, inverse)
    return (out, factor)


def solution(mesh):
    return jax.shard_map(
        shards,
        mesh=mesh,
        in_specs=(P(None, "partner", "blk"), P("partner"), P("blk", None), P(), P("blk"), P("blk")),
        out_specs=(P(None, "partner", "blk"), P("partner", None)),
        check_vma=False,
    )
```
